32 devices in a mesh: group: 2 (over x), feat: 8 (over z, y), layer: 2 (over core).
Axes of the slice: x: 2, y: 2, z: 4, core: 2. Of those that a mesh axis runs over, the one named last changes fastest.
Arguments:
- inputs: bfloat16 [2, 1024, 4096], P('layer', ('group', 'feat')), parts along dimension 1, may hold values from -6 to 6
- targets: bfloat16 [1024, 2, 4096], P(('group', 'feat'), None, 'layer'), parts along dimension 0, may hold values from -6 to 6
- tiles: int32 [2, 1024, 4], P('layer', 'group'), parts along dimension 1, may hold values from 0 to 127, as said below
- enc_weight: bfloat16 [2, 4096, 16384], P('layer', None, 'feat'), may hold values from -0.09375 to 0.09375
- enc_bias: bfloat16 [2, 16384], P('layer', 'feat'), may hold values from -3 to 3
- dec_weight: bfloat16 [2, 2, 16384, 4096], P('layer', None, 'feat'), may hold values from -0.25 to 0.25
- dec_bias: bfloat16 [2, 4096], P(None, 'layer'), may hold values from -3 to 3
Outputs:
- error: bfloat16 [1024, 2, 4096], P(('group', 'feat'), None, 'layer'), parts along dimension 0
The draws below stay inside these ranges and needn't reach their ends.
There are 2 independent parts, one for each index of `group`. The reference program is written for one: setup_inputs(seed, part) draws one part's arguments, and reference() takes and returns one part's arrays. A program takes and returns all parts, laid end to end along the dimension named above; an argument that names none is the same for every part. Nothing has to cross between parts.
Inputs may be any that keep to these rules, and one draw needn't show every extreme that they name: Each row lists 4 different tiles that lie in 4 different feature blocks of 16 consecutive tiles; among the 64 consecutive tokens of one index of feat, at most 32 rows list a tile of any one block, and in every such token block and source layer some feature block is listed by exactly 32 rows.
All inputs are finite; a program needn't handle non-finite values.
Results may differ from the reference program's by a relative error of at most 0.0085.
Values may be sent and summed in bfloat16 or wider, within the bound.
A program may use at most 128 MiB of HBM per device.

```python
import jax
import jax.numpy as jnp
from jax import lax

D = 4096
F = 16384
S = 2
NT = 2
KT = 4
TOK_DEV = 64
TOKENS = 512
NTILE = 128
N_FEAT = 8


def owner_tiles(key):
    owners = TOKENS // TOK_DEV
    per_block = NTILE // owners
    key_blocks, key_ranks, key_offsets = jax.random.split(key, 3)
    blocks = jax.random.permutation(key_blocks, owners).astype(jnp.int32)
    ranks = jax.random.permutation(key_ranks, TOK_DEV).astype(jnp.int32)
    slots = ranks[:, None] * KT + jnp.arange(KT, dtype=jnp.int32)[None, :]
    placed = blocks[slots % owners]
    offsets = jax.random.randint(key_offsets, (TOK_DEV, KT), 0, per_block).astype(jnp.int32)
    first_low = jnp.argmax(blocks == 0).astype(jnp.int32)
    first_high = jnp.argmax(blocks == owners - 1).astype(jnp.int32)
    offsets = jnp.where(slots == first_low, 0, offsets)
    offsets = jnp.where(slots == first_high, per_block - 1, offsets)
    return placed * per_block + offsets


def draw_tiles(key, part):
    key = jax.random.fold_in(key, 1)
    owners = TOKENS // TOK_DEV
    keys = jax.random.split(key, S * owners)
    drawn = jax.vmap(owner_tiles)(keys)
    return drawn.reshape(S, TOKENS, KT).astype(jnp.int32)


def block_levels(stream_key, extent, cuts, least, top_value):
    factor_of = 1.0
    for dim, shards_of in cuts:
        draws = jax.random.uniform(jax.random.fold_in(jax.random.fold_in(stream_key, 6), dim), (shards_of,), jnp.float32, least / len(cuts), top_value / len(cuts))
        factor_of = factor_of * jnp.repeat(jnp.exp(draws), extent[dim] // shards_of).reshape((-1,) + (1,) * (len(extent) - 1 - dim))
    return factor_of


def normal_values(own_key, extent, scale, reach, cuts=(), held_as=jnp.bfloat16):
    gain = block_levels(own_key, extent, cuts, -0.22, 0.18) if cuts else 1.0
    array = jax.random.normal(own_key, extent, jnp.float32) * scale * gain
    return jnp.minimum(jnp.maximum(array, -reach), reach).astype(held_as)


def setup_inputs(seed: int = 0, part: int = 0) -> dict:
    streams_of = jax.random.split(jax.random.key(seed), 8)
    own_keys = jax.random.split(jax.random.fold_in(streams_of[7], part), 8)
    return {
        "inputs": normal_values(own_keys[0], (S, TOKENS, D), 1.0, 6.0, ((0, 2), (1, 8))),
        "targets": normal_values(own_keys[1], (TOKENS, NT, D), 1.0, 6.0, ((0, 8), (2, 2))),
        "tiles": draw_tiles(jax.random.fold_in(jax.random.fold_in(streams_of[7], part), 71), part),
        "enc_weight": normal_values(streams_of[3], (S, D, F), D ** -0.5, 0.09375, ((0, 2), (2, 8))),
        "enc_bias": normal_values(streams_of[4], (S, F), 0.5, 3.0, ((0, 2), (1, 8))),
        "dec_weight": normal_values(streams_of[5], (S, NT, F, D), (KT * 128) ** -0.5, 0.25, ((0, 2), (2, 8))),
        "dec_bias": normal_values(streams_of[6], (NT, D), 0.5, 3.0, ((1, 2),)),
    }


def reference(inputs, targets, tiles, enc_weight, enc_bias, dec_weight, dec_bias):
    block_feats = F // N_FEAT
    tile_ids = jnp.arange(NTILE, dtype=jnp.int32)
    activations = []
    for source in range(S):
        preact = jnp.dot(inputs[source], enc_weight[source], preferred_element_type=jnp.float32)
        preact = preact + enc_bias[source].astype(jnp.float32)
        active = jnp.any(tiles[source][:, :, None] == tile_ids[None, None, :], axis=1)
        keep_mask = jnp.repeat(active, 128, axis=1)
        activations.append(jnp.where(keep_mask, jnp.maximum(preact, 0.0), 0.0).astype(jnp.bfloat16))
    results = []
    for target in range(NT):
        total = jnp.zeros((inputs.shape[1], D), jnp.float32)
        for source in range(S):
            if source <= target:
                for block in range(N_FEAT):
                    low = block * block_feats
                    partial_sum = jnp.dot(activations[source][:, low:low + block_feats],
                                          dec_weight[source, target, low:low + block_feats],
                                          preferred_element_type=jnp.float32).astype(jnp.bfloat16)
                    partial_sum = lax.optimization_barrier(partial_sum)
                    total = total + partial_sum.astype(jnp.float32)
        result = total + dec_bias[target].astype(jnp.float32) - targets[:, target].astype(jnp.float32)
        results.append(result.astype(jnp.bfloat16))
    return jnp.stack(results, axis=1)
```

```python
import functools

import jax
import jax.numpy as jnp
from jax import lax
from jax.experimental import pallas as pl
from jax.experimental.pallas import tpu as pltpu
from jax.sharding import PartitionSpec as P

MESH = pl.DeviceIdType.MESH
NY = 2
NK = 4
NJ = 4
BF = jnp.bfloat16
F32 = jnp.float32


def kernel(cfg, tt_ref, x_ref, bias_ref, we_ref, wd_ref, out_ref,
           wbuf, xcol, xp, ysend, acc, act, ppbuf, mbuf, cbuf, obuf, zacc, zown,
           w_sem, g_send, g_recv, y_send, y_recv, pp_send, pp_recv,
           e_send, e_recv, z_send, z_recv, o_recv):
    nz, tok, cap, th, width, feats = cfg
    f = lax.axis_index("feat")
    s = lax.axis_index("layer")
    z = lax.div(f, NY)
    y = lax.rem(f, NY)
    o = 1 - s
    f_par = z * NY + (1 - y)
    has_lo = z > 0
    has_hi = z < nz - 1
    kc = width // NK
    half = width // 2
    jc = half // NJ
    rows = nz * cap
    fh = feats // 2

    def w_copies(p, slot):
        if p < NK:
            return [pltpu.make_async_copy(
                we_ref.at[0, pl.ds(p * kc, kc), pl.ds(i * fh, fh)],
                wbuf.at[slot, pl.ds(i * kc, kc), :], w_sem.at[p, i]) for i in range(2)]
        j, t = (p - NK) // 2, (p - NK) % 2
        return [pltpu.make_async_copy(
            wd_ref.at[0, t, :, pl.ds(pl.multiple_of(h * half + j * jc, jc), jc)],
            wbuf.at[slot, :, pl.ds(i * jc, jc)], w_sem.at[p, i]) for i, h in enumerate((s, o))]

    def w_start(p):
        def go():
            for c in w_copies(p, p % 8):
                c.start()
        if p >= NK and (p - NK) % 2 == 0:
            pl.when(s == 0)(go)
        else:
            go()

    def w_wait(p):
        for c in w_copies(p, p % 8):
            c.wait()

    barrier = pltpu.get_barrier_semaphore()
    lo_id = {"feat": jnp.maximum(f - NY, 0)}
    hi_id = {"feat": jnp.minimum(f + NY, nz * NY - 1)}
    par_id = {"feat": f_par}
    core_id = {"layer": o}
    diag_id = {"feat": f_par, "layer": o}

    def greet(dev):
        pl.semaphore_signal(barrier, inc=1, device_id=dev, device_id_type=MESH)

    for dev in (par_id, core_id, diag_id):
        greet(dev)
    pl.when(has_lo)(lambda: greet(lo_id))
    pl.when(has_hi)(lambda: greet(hi_id))
    for p in range(8):
        w_start(p)
    pl.semaphore_wait(barrier, 3 + has_lo.astype(jnp.int32) + has_hi.astype(jnp.int32))

    def remote(src, dst, ss, rs, dev):
        return pltpu.make_async_remote_copy(
            src_ref=src, dst_ref=dst, send_sem=ss, recv_sem=rs,
            device_id=dev, device_id_type=MESH)

    def kcols(k):
        return pl.ds(pl.multiple_of(k * kc, kc), kc)

    def g_copy(src, zc, k, direction, dev):
        return remote(src.at[:, kcols(k)], xcol.at[zc, :, kcols(k)],
                      g_send.at[direction, zc, k], g_recv.at[zc, k], dev)

    for k in range(NK):
        pl.when(has_hi)(lambda: g_copy(x_ref, z, k, 0, hi_id).start())
        pl.when(has_lo)(lambda: g_copy(x_ref, z, k, 1, lo_id).start())

    blk = lax.div(tt_ref[...], th)
    ri = lax.broadcasted_iota(jnp.int32, (cap, 128), 0).astype(F32)
    tri = (lax.broadcasted_iota(jnp.int32, (128, 128), 0)
           <= lax.broadcasted_iota(jnp.int32, (128, 128), 1)).astype(F32)

    def picks(b, count):
        on = jnp.max(jnp.where(blk == b, 1.0, 0.0), axis=1)
        rank = jnp.dot(on, tri, preferred_element_type=F32) - 1.0
        return [jnp.where((ri == rank[q:q + 1]) & (on[q:q + 1] > 0.5), 1.0, 0.0).astype(BF)
                for q in range(count)]

    own = picks(f, nz * NY)
    par = picks(f_par, nz)
    for q in range(nz):
        ppbuf[0, q, 0:cap, :] = own[q]
        ppbuf[0, q, cap:2 * cap, :] = par[q]
    pp_copy = remote(ppbuf.at[0], ppbuf.at[1], pp_send, pp_recv, core_id)
    pp_copy.start()
    ti = lax.broadcasted_iota(jnp.int32, (th, 128), 0) + f * th
    for q in range(nz * NY):
        hit = jnp.zeros((th, 128), F32)
        for c in range(tt_ref.shape[1]):
            hit = jnp.where(tt_ref[q, c:c + 1, :] == ti, 1.0, hit)
        mbuf[q * cap:(q + 1) * cap, :] = lax.dot_general(
            own[q], hit.astype(BF), (((1,), (1,)), ((), ())), preferred_element_type=F32)
    acc[...] = jnp.broadcast_to(bias_ref[...].astype(F32), acc.shape)
    zero = jnp.zeros((rows, jc), BF)
    for i in range(2):
        for j in range(NJ):
            cbuf[2 * (1 - s) + i, j, 0] = zero

    def y_copy(zc, k):
        r = pl.ds(pl.multiple_of(rows + zc * cap, cap), cap)
        return remote(ysend.at[zc, :, kcols(k)], xp.at[r, kcols(k)],
                      y_send.at[zc, k], y_recv.at[zc, k], par_id)

    def pack(src, zc, k):
        v = jnp.dot(ppbuf[0, zc, :, 0:tok], src[:, kcols(k)],
                    preferred_element_type=F32).astype(BF)
        ysend[zc, :, kcols(k)] = v[cap:]
        y_copy(zc, k).start()
        xp[pl.ds(pl.multiple_of(zc * cap, cap), cap), kcols(k)] = v[:cap]

    def over_k(fn):
        def body(k, c):
            fn(k)
            return c
        lax.fori_loop(0, NK, body, 0)

    over_k(lambda k: pack(x_ref, z, k))

    for dist in range(1, nz):
        def step(k):
            def arrive(zc, direction, more, dev):
                g_copy(x_ref, zc, k, direction, dev).wait_recv()
                pl.when(more)(lambda: g_copy(xcol.at[zc], zc, k, direction, dev).start())
                pack(xcol.at[zc], zc, k)
            pl.when(z >= dist)(lambda: arrive(z - dist, 0, has_hi, hi_id))
            pl.when(z + dist < nz)(lambda: arrive(z + dist, 1, has_lo, lo_id))
        over_k(step)

    for k in range(NK):
        w_wait(k)
        for zc in range(nz):
            y_copy(zc, k).wait_recv()
        for i in range(2):
            def enc(n, c):
                dst = pl.ds(pl.multiple_of(i * fh + n * 256, 256), 256)
                acc[:, dst] += jnp.dot(
                    xp[:, k * kc:(k + 1) * kc],
                    wbuf[k, i * kc:(i + 1) * kc, pl.ds(pl.multiple_of(n * 256, 256), 256)],
                    preferred_element_type=F32)
                return c
            lax.fori_loop(0, fh // 256, enc, 0)
    for p in range(8, NK + 2 * NJ):
        w_start(p)
    for i in range(th):
        c = slice(i * 128, (i + 1) * 128)
        act[:, c] = jnp.where(mbuf[:, i:i + 1] > 0.5, jnp.maximum(acc[:, c], 0.0), 0.0).astype(BF)

    pp_copy.wait()
    ex = ((0, par_id), (1, core_id), (2, diag_id))

    def e_copy(m, dev, j, t):
        return remote(obuf.at[m, j, t], cbuf.at[m + 1, j, t],
                      e_send.at[m, j, t], e_recv.at[m, j, t], dev)

    def decode(j):
        for t in range(2):
            def go():
                p = NK + 2 * j + t
                w_wait(p)
                for h in range(2):
                    for n in range(jc // 256):
                        v = jnp.dot(act[...], wbuf[p % 8, :, h * jc + n * 256:h * jc + (n + 1) * 256],
                                    preferred_element_type=F32).astype(BF)
                        c = slice(n * 256, (n + 1) * 256)
                        if h == 0:
                            cbuf[0, j, t, :, c] = v[:rows]
                            obuf[0, j, t, :, c] = v[rows:]
                        else:
                            obuf[1, j, t, :, c] = v[:rows]
                            obuf[2, j, t, :, c] = v[rows:]
                for m, dev in ex:
                    e_copy(m, dev, j, t).start()
            if t == 0:
                pl.when(s == 0)(go)
            else:
                go()

    def part(d, j, t):
        sel = ppbuf[:, d, :, 0:tok].reshape(4 * cap, tok)
        r = pl.ds(pl.multiple_of(d * cap, cap), cap)
        v = cbuf[:, j, t, r, :].reshape(4 * cap, jc)
        return lax.dot_general(sel, v, (((0,), (0,)), ((), ())), preferred_element_type=F32)

    def z_copy(d, j, down, dev, last):
        dst = zown.at[j] if last else zacc.at[d, j]
        return remote(zacc.at[d, j], dst, z_send.at[d, j],
                      o_recv.at[j] if last else z_recv.at[d, j], dev)

    def line(j):
        for m, dev in ex:
            e_copy(m, dev, j, 1).wait_recv()
        pl.when(s == 0)(lambda: e_copy(0, par_id, j, 0).wait_recv())

        def others():
            e_copy(1, core_id, j, 0).wait_recv()
            e_copy(2, diag_id, j, 0).wait_recv()
        pl.when(s == 1)(others)
        for dist in range(nz - 1, 0, -1):
            def run(d, down, has_in, dev, in_dev):
                vs = [part(d, j, t) for t in range(2)]

                def first():
                    for t in range(2):
                        zacc[d, j, t] = vs[t].astype(BF)

                def add():
                    z_copy(d, j, down, in_dev, False).wait_recv()
                    for t in range(2):
                        zacc[d, j, t] = (vs[t] + zacc[d, j, t].astype(F32)).astype(BF)
                pl.when(has_in)(add)
                pl.when(jnp.logical_not(has_in))(first)
                z_copy(d, j, down, dev, down and dist == 1).start()
            pl.when(z >= dist)(lambda: run(z - dist, True, has_hi, lo_id, hi_id))
            pl.when(z + dist < nz)(lambda: run(z + dist, False, has_lo, hi_id, lo_id))

    decode(0)
    decode(1)
    for j in range(NJ):
        line(j)
        if j + 2 < NJ:
            decode(j + 2)
    for j in range(NJ):
        c = slice(j * jc, (j + 1) * jc)
        for t in range(2):
            out_ref[t, :, c] = part(z, j, t)

        def below():
            z_copy(z, j, False, lo_id, False).wait_recv()
            for t in range(2):
                out_ref[t, :, c] += zacc[z, j, t].astype(F32)

        def above():
            z_copy(z, j, True, hi_id, True).wait_recv()
            for t in range(2):
                out_ref[t, :, c] += zown[j, t].astype(F32)
        pl.when(has_lo)(below)
        pl.when(has_hi)(above)

    def sent(k):
        def up(zc):
            g_copy(x_ref, zc, k, 0, hi_id).wait_send()

        def down(zc):
            g_copy(x_ref, zc, k, 1, lo_id).wait_send()
        for zc in range(nz):
            pl.when(has_hi & (zc <= z))(lambda: up(zc))
            pl.when(has_lo & (zc >= z))(lambda: down(zc))
            y_copy(zc, k).wait_send()
    over_k(sent)
    for j in range(NJ):
        for m, dev in ex:
            e_copy(m, dev, j, 1).wait_send()

        def zero_t():
            for m, dev in ex:
                e_copy(m, dev, j, 0).wait_send()
        pl.when(s == 0)(zero_t)
        for d in range(nz):
            pl.when(z != d)(lambda: z_copy(d, j, True, lo_id, False).wait_send())


def fused(tt, x, bias, we, wd, nz):
    tok, width = x.shape
    feats = we.shape[2]
    th = feats // 128
    cap = tok * tt.shape[1] // (nz * NY)
    rows = nz * cap
    kc = width // NK
    jc = width // 2 // NJ
    dma = pltpu.SemaphoreType.DMA
    vmem = pl.BlockSpec(memory_space=pltpu.VMEM)
    hbm = pl.BlockSpec(memory_space=pl.ANY)
    return pl.pallas_call(
        functools.partial(kernel, (nz, tok, cap, th, width, feats)),
        out_shape=jax.ShapeDtypeStruct((2, tok, width // 2), F32),
        in_specs=[vmem, vmem, vmem, hbm, hbm],
        out_specs=vmem,
        scratch_shapes=[
            pltpu.VMEM((8, 2 * kc, feats // 2), BF),
            pltpu.VMEM((nz, tok, width), BF),
            pltpu.VMEM((2 * rows, width), BF),
            pltpu.VMEM((nz, cap, width), BF),
            pltpu.VMEM((2 * rows, feats), F32),
            pltpu.VMEM((2 * rows, feats), BF),
            pltpu.VMEM((2, nz, 2 * cap, 128), BF),
            pltpu.VMEM((2 * rows, th), F32),
            pltpu.VMEM((4, NJ, 2, rows, jc), BF),
            pltpu.VMEM((3, NJ, 2, rows, jc), BF),
            pltpu.VMEM((nz, NJ, 2, tok, jc), BF),
            pltpu.VMEM((NJ, 2, tok, jc), BF),
            dma((NK + 2 * NJ, 2)),
            dma((2, nz, NK)), dma((nz, NK)),
            dma((nz, NK)), dma((nz, NK)),
            dma, dma,
            dma((3, NJ, 2)), dma((3, NJ, 2)),
            dma((nz, NJ)), dma((nz, NJ)), dma((NJ,)),
        ],
        compiler_params=pltpu.CompilerParams(
            collective_id=0, has_side_effects=True, vmem_limit_bytes=58 * 2**20),
        cost_estimate=pl.CostEstimate(
            flops=2 * 2 * rows * feats * width * 3, bytes_accessed=48 * 2**20, transcendentals=0),
    )(tt, x, bias, we, wd)


def local_line(inputs, targets, tiles, enc_weight, enc_bias, dec_weight, dec_bias, *, nz):
    y = lax.axis_index("feat") % NY
    tok = inputs.shape[1]
    kt = tiles.shape[2]
    tt = tiles[0].T.reshape(kt, nz, NY, tok).transpose(2, 1, 0, 3)
    tt = jnp.where(y == 0, tt, tt[::-1]).reshape(nz * NY, kt, tok)
    tt = jnp.pad(tt, ((0, 0), (0, 0), (0, 128 - tok)), constant_values=-4096)
    recon = fused(tt, inputs[0], enc_bias, enc_weight, dec_weight, nz)
    result = (recon.transpose(1, 0, 2) + dec_bias.astype(F32)[None]
              - targets.astype(F32))
    return result.astype(BF)


def local_any(inputs, targets, tiles, enc_weight, enc_bias, dec_weight, dec_bias):
    source = lax.axis_index("layer")
    feat_index = lax.axis_index("feat")
    th = enc_weight.shape[2] // 128
    x = lax.all_gather(inputs[0], "feat", axis=0, tiled=True)
    pre = jnp.dot(x, enc_weight[0], preferred_element_type=F32) + enc_bias[0].astype(F32)
    ids = feat_index * th + jnp.arange(th, dtype=jnp.int32)
    active = jnp.any(tiles[0][:, :, None] == ids[None, None, :], axis=1)
    act = jnp.where(jnp.repeat(active, 128, axis=1), jnp.maximum(pre, 0.0), 0.0).astype(BF)
    columns = []
    for target in range(dec_weight.shape[1]):
        product = jnp.dot(act, dec_weight[0, target], preferred_element_type=F32)
        columns.append(product * (source <= target).astype(F32))
    both = jnp.stack(columns, axis=1).astype(BF)
    halves = lax.psum_scatter(both, "layer", scatter_dimension=2, tiled=True)
    summed = lax.psum_scatter(halves, "feat", scatter_dimension=0, tiled=True).astype(F32)
    result = summed + dec_bias.astype(F32)[None] - targets.astype(F32)
    return result.astype(BF)


def solution(mesh):
    nf = mesh.shape["feat"]
    local = functools.partial(local_line, nz=nf // NY) if nf == 8 else local_any
    return jax.shard_map(
        local,
        mesh=mesh,
        in_specs=(
            P("layer", ("group", "feat"), None),
            P(("group", "feat"), None, "layer"),
            P("layer", "group", None),
            P("layer", None, "feat"),
            P("layer", "feat"),
            P("layer", None, "feat", None),
            P(None, "layer"),
        ),
        out_specs=P(("group", "feat"), None, "layer"),
        check_vma=False,
    )
```

```python
import functools

import jax
import jax.numpy as jnp
from jax import lax
from jax.experimental import pallas as pl
from jax.experimental.pallas import tpu as pltpu
from jax.sharding import PartitionSpec as P

MESH = pl.DeviceIdType.MESH
NY = 2
NK = 4
NJ = 4
AHEAD = 3
NE = 4
ND = 4
BF = jnp.bfloat16
F32 = jnp.float32


def kernel(cfg, tt_ref, x_ref, bias_ref, we_ref, wd_ref, out_ref,
           wbuf, ttbuf, xcol, xp, ysend, acc, act, ppbuf, mbuf, cbuf, obuf, zacc, zown,
           w_sem, g_send, g_recv, y_send, y_recv, pp_send, pp_recv,
           e_send, e_recv, z_send, z_recv, o_recv):
    nz, tok, cap, th, width, feats = cfg
    f = lax.axis_index("feat")
    s = lax.axis_index("layer")
    z = lax.div(f, NY)
    y = lax.rem(f, NY)
    o = 1 - s
    f_par = z * NY + (1 - y)
    has_lo = z > 0
    has_hi = z < nz - 1
    kc = width // NK
    half = width // 2
    jc = half // NJ
    rows = nz * cap
    fh = feats // 2

    ke = width // NE
    per = NJ // ND

    def w_copies(p, slot):
        if p < NE:
            return [pltpu.make_async_copy(
                we_ref.at[0, pl.ds(p * ke, ke), pl.ds(i * fh, fh)],
                wbuf.at[slot, pl.ds(i * ke, ke), :], w_sem.at[p, i]) for i in range(2)]
        jw, t = (p - NE) // 2, (p - NE) % 2
        return [pltpu.make_async_copy(
            wd_ref.at[0, t, :, pl.ds(pl.multiple_of(h * half + (jw * per + m) * jc, jc), jc)],
            wbuf.at[slot, :, pl.ds((2 * m + i) * jc, jc)], w_sem.at[p, 2 * m + i])
            for m in range(per) for i, h in enumerate((s, o))]

    def w_start(p):
        def go():
            for c in w_copies(p, p % 8):
                c.start()
        if p >= NE and (p - NE) % 2 == 0:
            pl.when(s == 0)(go)
        else:
            go()

    def w_wait(p):
        for c in w_copies(p, p % 8):
            c.wait()

    barrier = pltpu.get_barrier_semaphore()
    lo_id = {"feat": jnp.maximum(f - NY, 0)}
    hi_id = {"feat": jnp.minimum(f + NY, nz * NY - 1)}
    par_id = {"feat": f_par}
    core_id = {"layer": o}
    diag_id = {"feat": f_par, "layer": o}

    def greet(dev):
        pl.semaphore_signal(barrier, inc=1, device_id=dev, device_id_type=MESH)

    for dev in (par_id, core_id, diag_id):
        greet(dev)
    pl.when(has_lo)(lambda: greet(lo_id))
    pl.when(has_hi)(lambda: greet(hi_id))
    for p in range(8):
        w_start(p)
    pl.semaphore_wait(barrier, 3 + has_lo.astype(jnp.int32) + has_hi.astype(jnp.int32))

    def remote(src, dst, ss, rs, dev):
        return pltpu.make_async_remote_copy(
            src_ref=src, dst_ref=dst, send_sem=ss, recv_sem=rs,
            device_id=dev, device_id_type=MESH)

    def kcols(k):
        return pl.ds(pl.multiple_of(k * kc, kc), kc)

    def g_copy(src, zc, k, direction, dev):
        return remote(src.at[:, kcols(k)], xcol.at[zc, :, kcols(k)],
                      g_send.at[direction, zc, k], g_recv.at[zc, k], dev)

    for k in range(NK):
        pl.when(has_hi)(lambda: g_copy(x_ref, z, k, 0, hi_id).start())
        pl.when(has_lo)(lambda: g_copy(x_ref, z, k, 1, lo_id).start())

    lane = lax.broadcasted_iota(jnp.int32, (tt_ref.shape[0], 128), 1)
    for zc in range(nz):
        t2 = tt_ref[:, zc * 128:(zc + 1) * 128]
        swapped = pltpu.roll(t2, 64, 1)
        ttbuf[zc] = jnp.where(lane < tok, jnp.where(y == 0, t2, swapped), -4096)
        ttbuf[nz + zc] = jnp.where(lane < tok, jnp.where(y == 0, swapped, t2), -4096)

    blk = lax.div(ttbuf[...], th)
    ri = lax.broadcasted_iota(jnp.int32, (cap, 128), 0).astype(F32)
    tri = (lax.broadcasted_iota(jnp.int32, (128, 128), 0)
           <= lax.broadcasted_iota(jnp.int32, (128, 128), 1)).astype(F32)

    def picks(b, count):
        on = jnp.max(jnp.where(blk == b, 1.0, 0.0), axis=1)
        rank = jnp.dot(on, tri, preferred_element_type=F32) - 1.0
        return [jnp.where((ri == rank[q:q + 1]) & (on[q:q + 1] > 0.5), 1.0, 0.0).astype(BF)
                for q in range(count)]

    own = picks(f, nz * NY)
    par = picks(f_par, nz)
    for q in range(nz):
        ppbuf[0, q, 0:cap, :] = own[q]
        ppbuf[0, q, cap:2 * cap, :] = par[q]
    pp_copy = remote(ppbuf.at[0], ppbuf.at[1], pp_send, pp_recv, core_id)
    pp_copy.start()
    ti = lax.broadcasted_iota(jnp.int32, (th, 128), 0) + f * th
    for q in range(nz * NY):
        hit = jnp.zeros((th, 128), F32)
        for c in range(tt_ref.shape[0]):
            hit = jnp.where(ttbuf[q, c:c + 1, :] == ti, 1.0, hit)
        mbuf[q * cap:(q + 1) * cap, :] = lax.dot_general(
            own[q], hit.astype(BF), (((1,), (1,)), ((), ())), preferred_element_type=F32)
    acc[...] = jnp.broadcast_to(bias_ref[...].astype(F32), acc.shape)
    zero = jnp.zeros((rows, jc), BF)
    for i in range(2):
        for j in range(NJ):
            cbuf[2 * (1 - s) + i, j, 0] = zero

    def y_copy(zc, k):
        r = pl.ds(pl.multiple_of(rows + zc * cap, cap), cap)
        return remote(ysend.at[zc, :, kcols(k)], xp.at[r, kcols(k)],
                      y_send.at[zc, k], y_recv.at[zc, k], par_id)

    def pack(src, zc, k):
        v = jnp.dot(ppbuf[0, zc, :, 0:tok], src[:, kcols(k)],
                    preferred_element_type=F32).astype(BF)
        ysend[zc, :, kcols(k)] = v[cap:]
        y_copy(zc, k).start()
        xp[pl.ds(pl.multiple_of(zc * cap, cap), cap), kcols(k)] = v[:cap]

    def over_k(fn):
        def body(k, c):
            fn(k)
            return c
        lax.fori_loop(0, NK, body, 0)

    over_k(lambda k: pack(x_ref, z, k))

    for dist in range(1, nz):
        def step(k):
            def arrive(zc, direction, more, dev):
                g_copy(x_ref, zc, k, direction, dev).wait_recv()
                pl.when(more)(lambda: g_copy(xcol.at[zc], zc, k, direction, dev).start())
                pack(xcol.at[zc], zc, k)
            pl.when(z >= dist)(lambda: arrive(z - dist, 0, has_hi, hi_id))
            pl.when(z + dist < nz)(lambda: arrive(z + dist, 1, has_lo, lo_id))
        if dist < nz - 1:
            over_k(step)

    def encode(e):
        w_wait(e)
        for k in range(e * NK // NE, (e + 1) * NK // NE):
            for zc in range(nz):
                y_copy(zc, k).wait_recv()
        for i in range(2):
            def enc(n, c):
                dst = pl.ds(pl.multiple_of(i * fh + n * 512, 512), 512)
                acc[:, dst] += jnp.dot(
                    xp[:, e * ke:(e + 1) * ke],
                    wbuf[e, i * ke:(i + 1) * ke, pl.ds(pl.multiple_of(n * 512, 512), 512)],
                    preferred_element_type=F32)
                return c
            lax.fori_loop(0, fh // 512, enc, 0)

    pk = NK // NE
    for k in range(NK):
        step(k)
        if k >= pk and k % pk == 0:
            encode(k // pk - 1)
    encode(NE - 1)
    for p in range(8, NE + 2 * ND):
        w_start(p)
    for i in range(th):
        c = slice(i * 128, (i + 1) * 128)
        act[:, c] = jnp.where(mbuf[:, i:i + 1] > 0.5, jnp.maximum(acc[:, c], 0.0), 0.0).astype(BF)

    pp_copy.wait()
    ex = ((0, par_id), (1, core_id), (2, diag_id))

    def e_copy(m, dev, j, t):
        return remote(obuf.at[m, j, t], cbuf.at[m + 1, j, t],
                      e_send.at[m, j, t], e_recv.at[m, j, t], dev)

    def decode(j):
        for t in range(2):
            def go():
                p = NE + 2 * (j // per) + t
                if j % per == 0:
                    w_wait(p)
                m0 = j % per * 2 * jc
                v = jnp.dot(act[...], wbuf[p % 8, :, m0:m0 + 2 * jc],
                            preferred_element_type=F32).astype(BF)
                cbuf[0, j, t] = v[:rows, :jc]
                obuf[0, j, t] = v[rows:, :jc]
                obuf[1, j, t] = v[:rows, jc:]
                obuf[2, j, t] = v[rows:, jc:]
                for m, dev in ex:
                    e_copy(m, dev, j, t).start()
            if t == 0:
                pl.when(s == 0)(go)
            else:
                go()

    def part(d, j, t):
        sel = ppbuf[:, d, :, 0:tok].reshape(4 * cap, tok)
        r = pl.ds(pl.multiple_of(d * cap, cap), cap)
        v = cbuf[:, j, t, r, :].reshape(4 * cap, jc)
        return lax.dot_general(sel, v, (((0,), (0,)), ((), ())), preferred_element_type=F32)

    def z_copy(d, j, down, dev, last):
        dst = zown.at[j] if last else zacc.at[d, j]
        return remote(zacc.at[d, j], dst, z_send.at[d, j],
                      o_recv.at[j] if last else z_recv.at[d, j], dev)

    def line(j):
        for m, dev in ex:
            e_copy(m, dev, j, 1).wait_recv()
        pl.when(s == 0)(lambda: e_copy(0, par_id, j, 0).wait_recv())

        def others():
            e_copy(1, core_id, j, 0).wait_recv()
            e_copy(2, diag_id, j, 0).wait_recv()
        pl.when(s == 1)(others)
        for dist in range(nz - 1, 0, -1):
            def run(d, down, has_in, dev, in_dev):
                vs = [part(d, j, t) for t in range(2)]

                def first():
                    for t in range(2):
                        zacc[d, j, t] = vs[t].astype(BF)

                def add():
                    z_copy(d, j, down, in_dev, False).wait_recv()
                    for t in range(2):
                        zacc[d, j, t] = (vs[t] + zacc[d, j, t].astype(F32)).astype(BF)
                pl.when(has_in)(add)
                pl.when(jnp.logical_not(has_in))(first)
                z_copy(d, j, down, dev, down and dist == 1).start()
            pl.when(z >= dist)(lambda: run(z - dist, True, has_hi, lo_id, hi_id))
            pl.when(z + dist < nz)(lambda: run(z + dist, False, has_lo, hi_id, lo_id))

    for j in range(AHEAD):
        decode(j)
    for j in range(NJ):
        line(j)
        if j + AHEAD < NJ:
            decode(j + AHEAD)
    for j in range(NJ):
        c = slice(j * jc, (j + 1) * jc)
        for t in range(2):
            out_ref[t, :, c] = part(z, j, t)

        def below():
            z_copy(z, j, False, lo_id, False).wait_recv()
            for t in range(2):
                out_ref[t, :, c] += zacc[z, j, t].astype(F32)

        def above():
            z_copy(z, j, True, hi_id, True).wait_recv()
            for t in range(2):
                out_ref[t, :, c] += zown[j, t].astype(F32)
        pl.when(has_lo)(below)
        pl.when(has_hi)(above)

    def sent(k):
        def up(zc):
            g_copy(x_ref, zc, k, 0, hi_id).wait_send()

        def down(zc):
            g_copy(x_ref, zc, k, 1, lo_id).wait_send()
        for zc in range(nz):
            pl.when(has_hi & (zc <= z))(lambda: up(zc))
            pl.when(has_lo & (zc >= z))(lambda: down(zc))
            y_copy(zc, k).wait_send()
    over_k(sent)
    for j in range(NJ):
        for m, dev in ex:
            e_copy(m, dev, j, 1).wait_send()

        def zero_t():
            for m, dev in ex:
                e_copy(m, dev, j, 0).wait_send()
        pl.when(s == 0)(zero_t)
        for d in range(nz):
            pl.when(z != d)(lambda: z_copy(d, j, True, lo_id, False).wait_send())


def fused(tt, x, bias, we, wd, nz):
    tok, width = x.shape
    feats = we.shape[2]
    th = feats // 128
    cap = tok * tt.shape[0] // (nz * NY)
    rows = nz * cap
    jc = width // 2 // NJ
    dma = pltpu.SemaphoreType.DMA
    vmem = pl.BlockSpec(memory_space=pltpu.VMEM)
    hbm = pl.BlockSpec(memory_space=pl.ANY)
    return pl.pallas_call(
        functools.partial(kernel, (nz, tok, cap, th, width, feats)),
        out_shape=jax.ShapeDtypeStruct((2, tok, width // 2), F32),
        in_specs=[vmem, vmem, vmem, hbm, hbm],
        out_specs=vmem,
        scratch_shapes=[
            pltpu.VMEM((8, 2 * (width // NE), feats // 2), BF),
            pltpu.VMEM((nz * NY, tt.shape[0], 128), jnp.int32),
            pltpu.VMEM((nz, tok, width), BF),
            pltpu.VMEM((2 * rows, width), BF),
            pltpu.VMEM((nz, cap, width), BF),
            pltpu.VMEM((2 * rows, feats), F32),
            pltpu.VMEM((2 * rows, feats), BF),
            pltpu.VMEM((2, nz, 2 * cap, 128), BF),
            pltpu.VMEM((2 * rows, th), F32),
            pltpu.VMEM((4, NJ, 2, rows, jc), BF),
            pltpu.VMEM((3, NJ, 2, rows, jc), BF),
            pltpu.VMEM((nz, NJ, 2, tok, jc), BF),
            pltpu.VMEM((NJ, 2, tok, jc), BF),
            dma((NE + 2 * ND, 2 * NJ // ND)),
            dma((2, nz, NK)), dma((nz, NK)),
            dma((nz, NK)), dma((nz, NK)),
            dma, dma,
            dma((3, NJ, 2)), dma((3, NJ, 2)),
            dma((nz, NJ)), dma((nz, NJ)), dma((NJ,)),
        ],
        compiler_params=pltpu.CompilerParams(
            collective_id=0, has_side_effects=True, vmem_limit_bytes=58 * 2**20),
        cost_estimate=pl.CostEstimate(
            flops=2 * 2 * rows * feats * width * 3, bytes_accessed=48 * 2**20, transcendentals=0),
    )(tt, x, bias, we, wd)


def local_line(inputs, targets, tiles, enc_weight, enc_bias, dec_weight, dec_bias, *, nz):
    tt = tiles[0].T
    recon = fused(tt, inputs[0], enc_bias, enc_weight, dec_weight, nz)
    result = (recon.transpose(1, 0, 2) + dec_bias.astype(F32)[None]
              - targets.astype(F32))
    return result.astype(BF)


def local_any(inputs, targets, tiles, enc_weight, enc_bias, dec_weight, dec_bias):
    source = lax.axis_index("layer")
    feat_index = lax.axis_index("feat")
    th = enc_weight.shape[2] // 128
    x = lax.all_gather(inputs[0], "feat", axis=0, tiled=True)
    pre = jnp.dot(x, enc_weight[0], preferred_element_type=F32) + enc_bias[0].astype(F32)
    ids = feat_index * th + jnp.arange(th, dtype=jnp.int32)
    active = jnp.any(tiles[0][:, :, None] == ids[None, None, :], axis=1)
    act = jnp.where(jnp.repeat(active, 128, axis=1), jnp.maximum(pre, 0.0), 0.0).astype(BF)
    columns = []
    for target in range(dec_weight.shape[1]):
        product = jnp.dot(act, dec_weight[0, target], preferred_element_type=F32)
        columns.append(product * (source <= target).astype(F32))
    both = jnp.stack(columns, axis=1).astype(BF)
    halves = lax.psum_scatter(both, "layer", scatter_dimension=2, tiled=True)
    summed = lax.psum_scatter(halves, "feat", scatter_dimension=0, tiled=True).astype(F32)
    result = summed + dec_bias.astype(F32)[None] - targets.astype(F32)
    return result.astype(BF)


def solution(mesh):
    nf = mesh.shape["feat"]
    local = functools.partial(local_line, nz=nf // NY) if nf == 8 else local_any
    return jax.shard_map(
        local,
        mesh=mesh,
        in_specs=(
            P("layer", ("group", "feat"), None),
            P(("group", "feat"), None, "layer"),
            P("layer", "group", None),
            P("layer", None, "feat"),
            P("layer", "feat"),
            P("layer", None, "feat", None),
            P(None, "layer"),
        ),
        out_specs=P(("group", "feat"), None, "layer"),
        check_vma=False,
    )
```
